32 devices in a mesh: wide: 8 (over z, core), narrow: 4 (over y, x).
Axes of the slice: x: 2, y: 2, z: 4, core: 2. Of those that a mesh axis runs over, the one named last changes fastest.
Arguments:
- query_left: float32 [288, 4, 8, 5120], P('wide', 'narrow'), may hold values from -0.078125 to 0.078125
- query_right: float32 [288, 8, 13824], P('wide', None, 'narrow'), may hold values from -0.0017089844 to 0.0017089844
- acts: bfloat16 [8, 128, 5120], P('wide'), may hold values from -6 to 6
- grads: bfloat16 [8, 128, 13824], P('wide', None, 'narrow'), may hold values from -6 to 6
- order: int32 [8], replicated, may hold values from 0 to 7, each once
Outputs:
- scores: float32 [288, 8], P('wide')
The draws below stay inside these ranges and needn't reach their ends.
Inputs may be any that keep to these rules, and one draw needn't show every extreme that they name: order names every training example exactly once.
All inputs are finite; a program needn't handle non-finite values.
Results may differ from the reference program's by a relative error of at most 0.0003.
Values may be sent and summed in bfloat16 or wider, within the bound.
A program may use at most 64 MiB of HBM per device.

```python
import jax
import jax.numpy as jnp
from jax import lax

D = 5120
FF = 13824
RANK = 8
SEQ = 128
QUERIES = 288
EXAMPLES = 8
N_NARROW = 4


def block_scale(stream_key, dims, pieces, smallest, high):
    def one(axis_at, blocks):
        steps = jax.random.uniform(jax.random.fold_in(jax.random.fold_in(stream_key, 6), axis_at), (blocks,), jnp.float32, smallest / len(pieces), high / len(pieces))
        return jnp.repeat(jnp.exp(steps), dims[axis_at] // blocks).reshape((-1,) + (1,) * (len(dims) - axis_at - 1))

    level = one(*pieces[0])
    for cut in pieces[1:]:
        level = level * one(*cut)
    return level


def noise(rng, shape, scale, limit, shards=(), kind=jnp.bfloat16):
    loudness = block_scale(rng, shape, shards, -0.22, 0.18) if shards else 1.0
    array = jax.random.normal(rng, shape, jnp.float32) * scale * loudness
    return jnp.minimum(jnp.maximum(array, -limit), limit).astype(kind)


def setup_inputs(seed: int = 0) -> dict:
    arg_keys = jax.random.split(jax.random.key(seed), 6)
    return {
        "query_left": noise(arg_keys[0], (QUERIES, N_NARROW, RANK, D), D ** -0.5, 0.078125, ((0, 8), (1, 4)), jnp.float32),
        "query_right": noise(arg_keys[1], (QUERIES, RANK, FF), (FF * RANK * SEQ) ** -0.5, 0.0017089844, ((0, 8), (2, 4)), jnp.float32),
        "acts": noise(arg_keys[2], (EXAMPLES, SEQ, D), 1.0, 6.0, ((0, 8),)),
        "grads": noise(arg_keys[3], (EXAMPLES, SEQ, FF), 1.0, 6.0, ((0, 8), (2, 4))),
        "order": jax.random.permutation(arg_keys[4], EXAMPLES).astype(jnp.int32),
    }


def reference(query_left, query_right, acts, grads, order):
    blocks = query_left.shape[1]
    width = query_right.shape[2] // blocks
    right = query_right.reshape(query_right.shape[0], query_right.shape[1], blocks, width)

    def single(pair):
        act_one, grad_one = pair
        act_full = act_one.astype(jnp.float32)
        grad_full = grad_one.astype(jnp.float32).reshape(act_one.shape[0], blocks, width)
        left_proj = jnp.einsum("qbrd,sd->qbrs", query_left, act_full, precision=lax.Precision.HIGHEST)
        right_proj = jnp.einsum("qrbk,sbk->qbrs", right, grad_full, precision=lax.Precision.HIGHEST)
        return jnp.sum(left_proj * right_proj, axis=(1, 2, 3))

    raw = lax.map(single, (acts, grads))
    return jnp.transpose(raw)[:, order]
```

```python
import functools

import jax
import jax.numpy as jnp
from jax import lax
from jax.experimental import pallas as pl
from jax.experimental.pallas import tpu as pltpu
from jax.sharding import PartitionSpec as P

CORES = 2
CHUNKS = 4
MESH = pl.DeviceIdType.MESH


def kernel(
    levels, narrow, left_hbm, right_hbm, acts_hbm, grads_hbm, raw_out,
    acts_all, grads_all, left_in, right_in, left_two, right_two, x_ref, total, parts,
    load_sem, za_send, za_recv, zg_send, zg_recv, pa_send, pa_recv,
    ca_send, ca_recv, cg_send, cg_recv, sum_send, sum_recv,
):
    wide_at = lax.axis_index("wide")
    me = lax.axis_index("narrow")
    z = lax.div(wide_at, CORES)
    core = lax.rem(wide_at, CORES)
    other = z * CORES + (1 - core)
    tokens, width = acts_hbm.shape[1:]
    rows = left_hbm.shape[0]
    queries = raw_out.shape[0]
    ranks = rows // queries

    row_parts = min(narrow, tokens // 16)
    col_parts = narrow // row_parts
    piece_rows, piece_cols = tokens // row_parts, width // col_parts
    chunk_rows = tokens // CHUNKS

    def piece(n):
        row = pl.multiple_of(lax.rem(n, row_parts) * piece_rows, piece_rows)
        if col_parts == 1:
            return (pl.ds(row, piece_rows), slice(None))
        col = pl.multiple_of(lax.div(n, row_parts) * piece_cols, piece_cols)
        return (pl.ds(row, piece_rows), pl.ds(col, piece_cols))

    def acts_at(example, n):
        return acts_all.at[(example, *piece(n))]

    def grads_at(example, g):
        return grads_all.at[example, pl.ds(g * chunk_rows, chunk_rows), :]

    def send(src, dst, send_sem, recv_sem, **where):
        return pltpu.make_async_remote_copy(
            src_ref=src, dst_ref=dst, send_sem=send_sem, recv_sem=recv_sem,
            device_id=where, device_id_type=MESH,
        )

    def z_acts(level, way, target, src=None):
        slot = acts_at(level * CORES + core, me)
        return send(slot if src is None else src, slot, za_send.at[level, way], za_recv.at[level], wide=target)

    def z_grads(level, way, target, g, src=None):
        slot = grads_at(level * CORES + core, g)
        return send(slot if src is None else src, slot, zg_send.at[level, way, g], zg_recv.at[level, g], wide=target)

    def plane_acts(level, n, target):
        slot = acts_at(level * CORES + core, n)
        return send(slot, slot, pa_send.at[level, target], pa_recv.at[level, n], narrow=target)

    def core_acts(level, n, whose, src=None):
        slot = acts_at(level * CORES + whose, n)
        return send(slot if src is None else src, slot, ca_send.at[level, n], ca_recv.at[level, n], wide=other)

    def core_grads(level, g, whose, src=None):
        slot = grads_at(level * CORES + whose, g)
        return send(slot if src is None else src, slot, cg_send.at[level, g], cg_recv.at[level, g], wide=other)

    barrier = pltpu.get_barrier_semaphore()
    up, down = z + 1 < levels, z > 0

    @pl.when(up)
    def _():
        pl.semaphore_signal(barrier, inc=1, device_id={"wide": wide_at + CORES}, device_id_type=MESH)

    @pl.when(down)
    def _():
        pl.semaphore_signal(barrier, inc=1, device_id={"wide": wide_at - CORES}, device_id_type=MESH)

    pl.semaphore_signal(barrier, inc=1, device_id={"wide": other}, device_id_type=MESH)
    for j in range(1, narrow):
        pl.semaphore_signal(barrier, inc=1, device_id={"narrow": lax.rem(me + j, narrow)}, device_id_type=MESH)
    pl.semaphore_wait(barrier, narrow + up.astype(jnp.int32) + down.astype(jnp.int32))

    own_acts = acts_hbm.at[(0, *piece(me))]

    def own_grads(g):
        return grads_hbm.at[0, pl.ds(g * chunk_rows, chunk_rows), :]

    for way, ok in ((0, up), (1, down)):
        target = wide_at + (CORES if way == 0 else -CORES)

        @pl.when(ok)
        def _():
            z_acts(z, way, target, own_acts).start()
            for g in range(CHUNKS):
                z_grads(z, way, target, g, own_grads(g)).start()

    for n in range(narrow):
        core_acts(z, n, core, acts_hbm.at[(0, *piece(n))]).start()
    for g in range(CHUNKS):
        core_grads(z, g, core, own_grads(g)).start()

    loads = [
        pltpu.make_async_copy(left_hbm, left_in, load_sem.at[0]),
        pltpu.make_async_copy(right_hbm, right_in, load_sem.at[1]),
        pltpu.make_async_copy(acts_hbm.at[0], acts_all.at[wide_at], load_sem.at[2]),
        pltpu.make_async_copy(grads_hbm.at[0], grads_all.at[wide_at], load_sem.at[3]),
    ]
    for load in loads:
        load.start()
    total[...] = jnp.zeros_like(total)

    def split(src, dst):
        def step(i, carry):
            row = pl.multiple_of(i * 32, 32)
            value = src[pl.ds(row, 32), :]
            high = value.astype(jnp.bfloat16)
            dst[pl.ds(row, 32), :] = high
            dst[pl.ds(rows + row, 32), :] = (value - high.astype(jnp.float32)).astype(jnp.bfloat16)
            return carry

        lax.fori_loop(0, rows // 32, step, 0)

    loads[0].wait()
    split(left_in, left_two)
    loads[1].wait()
    split(right_in, right_two)
    loads[2].wait()
    loads[3].wait()

    def project(two, ref, level):
        block = ref[pl.ds(level * CORES, CORES)]
        block = block.reshape(CORES * tokens, block.shape[2])
        both = lax.dot_general(two[...], block, (((1,), (1,)), ((), ())), preferred_element_type=jnp.float32)
        return both[:rows] + both[rows:]

    def work(level):
        for n in range(narrow):
            core_acts(level, n, 1 - core).wait_recv()
        x_ref[...] = project(left_two, acts_all, level)
        for g in range(CHUNKS):
            core_grads(level, g, 1 - core).wait_recv()
        product = x_ref[...] * project(right_two, grads_all, level)
        by_query = jnp.sum(product.reshape(queries, ranks, CORES * tokens), axis=1)
        column = lax.broadcasted_iota(jnp.int32, total.shape, 1)
        for c in range(CORES):
            score = jnp.sum(by_query[:, c * tokens:(c + 1) * tokens], axis=1, keepdims=True)
            total[...] += jnp.where(column == level * CORES + c, score, 0.0)

    def step(i, carry):
        way = lax.rem(i, 2)
        sign = 1 - 2 * way
        level = z - sign * (lax.div(i, 2) + 1)
        following = z + sign

        @pl.when(jnp.logical_and(level >= 0, level < levels))
        def _():
            onward = jnp.logical_and(following >= 0, following < levels)
            target = following * CORES + core
            z_acts(level, way, wide_at).wait_recv()

            @pl.when(onward)
            def _():
                z_acts(level, way, target).start()

            for j in range(1, narrow):
                plane_acts(level, me, lax.rem(me + j, narrow)).start()
            core_acts(level, me, core).start()
            for g in range(CHUNKS):
                z_grads(level, way, wide_at, g).wait_recv()

                @pl.when(onward)
                def _():
                    z_grads(level, way, target, g).start()

                core_grads(level, g, core).start()
            for j in range(1, narrow):
                n = lax.rem(me + j, narrow)
                plane_acts(level, n, me).wait_recv()
                core_acts(level, n, core).start()
            work(level)

        return carry

    work(z)
    lax.fori_loop(0, 2 * (levels - 1), step, 0)

    parts[me] = total[...]

    def sums(target, n):
        return send(total, parts.at[n], sum_send.at[target], sum_recv.at[n], narrow=target)

    for j in range(1, narrow):
        sums(lax.rem(me + j, narrow), me).start()

    for n in range(narrow):
        core_acts(z, n, core).wait_send()
    for g in range(CHUNKS):
        core_grads(z, g, core).wait_send()
    for way, ok in ((0, up), (1, down)):
        target = wide_at + (CORES if way == 0 else -CORES)

        @pl.when(ok)
        def _():
            z_acts(z, way, target).wait_send()
            for g in range(CHUNKS):
                z_grads(z, way, target, g).wait_send()

    def drain(i, carry):
        way = lax.rem(i, 2)
        sign = 1 - 2 * way
        level = z - sign * (lax.div(i, 2) + 1)
        following = z + sign

        @pl.when(jnp.logical_and(level >= 0, level < levels))
        def _():
            @pl.when(jnp.logical_and(following >= 0, following < levels))
            def _():
                target = following * CORES + core
                z_acts(level, way, target).wait_send()
                for g in range(CHUNKS):
                    z_grads(level, way, target, g).wait_send()

            for j in range(1, narrow):
                plane_acts(level, me, lax.rem(me + j, narrow)).wait_send()
            for n in range(narrow):
                core_acts(level, n, core).wait_send()
            for g in range(CHUNKS):
                core_grads(level, g, core).wait_send()

        return carry

    lax.fori_loop(0, 2 * (levels - 1), drain, 0)
    for j in range(1, narrow):
        sums(me, lax.rem(me + j, narrow)).wait_recv()
    raw = parts[0]
    for n in range(1, narrow):
        raw += parts[n]
    raw_out[...] = raw
    for j in range(1, narrow):
        sums(lax.rem(me + j, narrow), me).wait_send()


def body(query_left, query_right, acts, grads, order):
    queries, _, ranks, width = query_left.shape
    block = query_right.shape[2]
    rows = queries * ranks
    owners, narrow = lax.axis_size("wide"), lax.axis_size("narrow")
    levels = owners // CORES
    tokens = acts.shape[1]
    dma = pltpu.SemaphoreType.DMA
    hbm = pl.BlockSpec(memory_space=pl.ANY)
    raw = pl.pallas_call(
        functools.partial(kernel, levels, narrow),
        out_shape=jax.ShapeDtypeStruct((queries, 128), jnp.float32),
        in_specs=[hbm] * 4,
        out_specs=pl.BlockSpec(memory_space=pltpu.VMEM),
        scratch_shapes=[
            pltpu.VMEM((owners, tokens, width), jnp.bfloat16),
            pltpu.VMEM((owners, tokens, block), jnp.bfloat16),
            pltpu.VMEM((rows, width), jnp.float32),
            pltpu.VMEM((rows, block), jnp.float32),
            pltpu.VMEM((2 * rows, width), jnp.bfloat16),
            pltpu.VMEM((2 * rows, block), jnp.bfloat16),
            pltpu.VMEM((rows, CORES * tokens), jnp.float32),
            pltpu.VMEM((queries, 128), jnp.float32),
            pltpu.VMEM((narrow, queries, 128), jnp.float32),
            dma((4,)),
            dma((levels, 2)), dma((levels,)),
            dma((levels, 2, CHUNKS)), dma((levels, CHUNKS)),
            dma((levels, narrow)), dma((levels, narrow)),
            dma((levels, narrow)), dma((levels, narrow)),
            dma((levels, CHUNKS)), dma((levels, CHUNKS)),
            dma((narrow,)), dma((narrow,)),
        ],
        compiler_params=pltpu.CompilerParams(
            collective_id=0, has_side_effects=True, vmem_limit_bytes=58 * 1024 * 1024,
        ),
        cost_estimate=pl.CostEstimate(
            flops=4 * rows * owners * tokens * (width + block),
            bytes_accessed=4 * rows * (width + block), transcendentals=0,
        ),
        name="scores",
    )(
        query_left.reshape(rows, width),
        query_right.reshape(rows, block),
        acts,
        grads,
    )
    picker = (lax.broadcasted_iota(jnp.int32, (owners, owners), 0) == order[None, :]).astype(jnp.float32)
    return jnp.sum(raw[:, :owners, None] * picker[None], axis=1)


def solution(mesh):
    return jax.shard_map(
        body,
        mesh=mesh,
        in_specs=(
            P("wide", "narrow", None, None),
            P("wide", None, "narrow"),
            P("wide", None, None),
            P("wide", None, "narrow"),
            P(),
        ),
        out_specs=P("wide", None),
        check_vma=False,
    )
```

```python
import functools

import jax
import jax.numpy as jnp
from jax import lax
from jax.experimental import pallas as pl
from jax.experimental.pallas import tpu as pltpu
from jax.sharding import PartitionSpec as P

CORES = 2
CHUNKS = 4
MESH = pl.DeviceIdType.MESH


def kernel(
    levels, narrow, left_hbm, right_hbm, acts_hbm, grads_hbm, raw_out,
    acts_all, grads_all, left_in, right_in, left_two, right_two, x_ref, total, parts,
    load_sem, za_send, za_recv, zg_send, zg_recv, pa_send, pa_recv,
    ca_send, ca_recv, cg_send, cg_recv, sum_send, sum_recv,
):
    wide_at = lax.axis_index("wide")
    me = lax.axis_index("narrow")
    z = lax.div(wide_at, CORES)
    core = lax.rem(wide_at, CORES)
    other = z * CORES + (1 - core)
    tokens, width = acts_hbm.shape[1:]
    rows = left_hbm.shape[0]
    queries = raw_out.shape[0]
    ranks = rows // queries

    row_parts = min(narrow, tokens // 16)
    col_parts = narrow // row_parts
    piece_rows, piece_cols = tokens // row_parts, width // col_parts
    chunk_rows = tokens // CHUNKS

    def piece(n):
        row = pl.multiple_of(lax.rem(n, row_parts) * piece_rows, piece_rows)
        if col_parts == 1:
            return (pl.ds(row, piece_rows), slice(None))
        col = pl.multiple_of(lax.div(n, row_parts) * piece_cols, piece_cols)
        return (pl.ds(row, piece_rows), pl.ds(col, piece_cols))

    def acts_at(example, n):
        return acts_all.at[(example, *piece(n))]

    def grads_at(example, g):
        return grads_all.at[example, pl.ds(g * chunk_rows, chunk_rows), :]

    def send(src, dst, send_sem, recv_sem, **where):
        return pltpu.make_async_remote_copy(
            src_ref=src, dst_ref=dst, send_sem=send_sem, recv_sem=recv_sem,
            device_id=where, device_id_type=MESH,
        )

    def z_acts(level, way, target, src=None):
        slot = acts_at(level * CORES + core, me)
        return send(slot if src is None else src, slot, za_send.at[level, way], za_recv.at[level], wide=target)

    def z_grads(level, way, target, g, src=None):
        slot = grads_at(level * CORES + core, g)
        return send(slot if src is None else src, slot, zg_send.at[level, way, g], zg_recv.at[level, g], wide=target)

    def plane_acts(level, n, target):
        slot = acts_at(level * CORES + core, n)
        return send(slot, slot, pa_send.at[level, target], pa_recv.at[level, n], narrow=target)

    def core_acts(level, n, whose, src=None):
        slot = acts_at(level * CORES + whose, n)
        return send(slot if src is None else src, slot, ca_send.at[level, n], ca_recv.at[level, n], wide=other)

    def core_grads(level, g, whose, src=None):
        slot = grads_at(level * CORES + whose, g)
        return send(slot if src is None else src, slot, cg_send.at[level, g], cg_recv.at[level, g], wide=other)

    barrier = pltpu.get_barrier_semaphore()
    up, down = z + 1 < levels, z > 0

    @pl.when(up)
    def _():
        pl.semaphore_signal(barrier, inc=1, device_id={"wide": wide_at + CORES}, device_id_type=MESH)

    @pl.when(down)
    def _():
        pl.semaphore_signal(barrier, inc=1, device_id={"wide": wide_at - CORES}, device_id_type=MESH)

    pl.semaphore_signal(barrier, inc=1, device_id={"wide": other}, device_id_type=MESH)
    for j in range(1, narrow):
        pl.semaphore_signal(barrier, inc=1, device_id={"narrow": lax.rem(me + j, narrow)}, device_id_type=MESH)
    pl.semaphore_wait(barrier, narrow + up.astype(jnp.int32) + down.astype(jnp.int32))

    own_acts = acts_hbm.at[(0, *piece(me))]

    def own_grads(g):
        return grads_hbm.at[0, pl.ds(g * chunk_rows, chunk_rows), :]

    for way, ok in ((0, up), (1, down)):
        target = wide_at + (CORES if way == 0 else -CORES)

        @pl.when(ok)
        def _():
            z_acts(z, way, target, own_acts).start()
            for g in range(CHUNKS):
                z_grads(z, way, target, g, own_grads(g)).start()

    for n in range(narrow):
        core_acts(z, n, core, acts_hbm.at[(0, *piece(n))]).start()
    for g in range(CHUNKS):
        core_grads(z, g, core, own_grads(g)).start()

    loads = [
        pltpu.make_async_copy(left_hbm, left_in, load_sem.at[0]),
        pltpu.make_async_copy(right_hbm, right_in, load_sem.at[1]),
        pltpu.make_async_copy(acts_hbm.at[0], acts_all.at[wide_at], load_sem.at[2]),
        pltpu.make_async_copy(grads_hbm.at[0], grads_all.at[wide_at], load_sem.at[3]),
    ]
    for load in loads:
        load.start()
    total[...] = jnp.zeros_like(total)

    def split(src, dst):
        def step(i, carry):
            row = pl.multiple_of(i * 32, 32)
            value = src[pl.ds(row, 32), :]
            high = value.astype(jnp.bfloat16)
            dst[pl.ds(row, 32), :] = high
            dst[pl.ds(rows + row, 32), :] = (value - high.astype(jnp.float32)).astype(jnp.bfloat16)
            return carry

        lax.fori_loop(0, rows // 32, step, 0)

    loads[0].wait()
    split(left_in, left_two)
    loads[1].wait()
    split(right_in, right_two)
    loads[2].wait()
    loads[3].wait()

    def project(two, ref, level):
        block = ref[pl.ds(level * CORES, CORES)]
        block = block.reshape(CORES * tokens, block.shape[2])
        both = lax.dot_general(two[...], block, (((1,), (1,)), ((), ())), preferred_element_type=jnp.float32)
        return both[:rows] + both[rows:]

    def left_work(level, way):
        for n in range(narrow):
            core_acts(level, n, 1 - core).wait_recv()
        x_ref[way] = project(left_two, acts_all, level)

    def right_work(level, way):
        for g in range(CHUNKS):
            core_grads(level, g, 1 - core).wait_recv()
        product = x_ref[way] * project(right_two, grads_all, level)
        by_query = jnp.sum(product.reshape(queries, ranks, CORES * tokens), axis=1)
        column = lax.broadcasted_iota(jnp.int32, total.shape, 1)
        for c in range(CORES):
            score = jnp.sum(by_query[:, c * tokens:(c + 1) * tokens], axis=1, keepdims=True)
            total[...] += jnp.where(column == level * CORES + c, score, 0.0)

    def arrivals(d):
        found = []
        for way, sign in ((0, 1), (1, -1)):
            level, following = z - sign * d, z + sign
            valid = jnp.logical_and(level >= 0, level < levels)
            onward = jnp.logical_and(following >= 0, following < levels)
            found.append((way, level, valid, jnp.logical_and(valid, onward), following * CORES + core))
        return found

    def take_grads(now, g):
        for way, level, valid, onward, target in now:
            @pl.when(valid)
            def _():
                z_grads(level, way, wide_at, g).wait_recv()

            @pl.when(onward)
            def _():
                z_grads(level, way, target, g).start()

            @pl.when(valid)
            def _():
                core_grads(level, g, core).start()

    def step(i, carry):
        now, before = arrivals(i + 1), arrivals(i)
        for way, level, valid, onward, target in now:
            @pl.when(valid)
            def _():
                z_acts(level, way, wide_at).wait_recv()

            @pl.when(onward)
            def _():
                z_acts(level, way, target).start()

            @pl.when(valid)
            def _():
                for j in range(1, narrow):
                    plane_acts(level, me, lax.rem(me + j, narrow)).start()
                core_acts(level, me, core).start()

        take_grads(now, 0)
        for way, level, valid, _, _ in before:
            @pl.when(jnp.logical_and(valid, i > 0))
            def _():
                right_work(level, way)

        take_grads(now, 1)
        for way, level, valid, _, _ in now:
            @pl.when(valid)
            def _():
                for j in range(1, narrow):
                    n = lax.rem(me + j, narrow)
                    plane_acts(level, n, me).wait_recv()
                    core_acts(level, n, core).start()

        take_grads(now, 2)
        for way, level, valid, _, _ in now:
            @pl.when(valid)
            def _():
                left_work(level, way)

        for g in range(3, CHUNKS):
            take_grads(now, g)
        return carry

    left_work(z, 0)
    right_work(z, 0)
    lax.fori_loop(0, levels - 1, step, 0)
    for way, level, valid, _, _ in arrivals(levels - 1):
        @pl.when(valid)
        def _():
            right_work(level, way)

    parts[me] = total[...]

    def sums(target, n):
        return send(total, parts.at[n], sum_send.at[target], sum_recv.at[n], narrow=target)

    for j in range(1, narrow):
        sums(lax.rem(me + j, narrow), me).start()

    for n in range(narrow):
        core_acts(z, n, core).wait_send()
    for g in range(CHUNKS):
        core_grads(z, g, core).wait_send()
    for way, ok in ((0, up), (1, down)):
        target = wide_at + (CORES if way == 0 else -CORES)

        @pl.when(ok)
        def _():
            z_acts(z, way, target).wait_send()
            for g in range(CHUNKS):
                z_grads(z, way, target, g).wait_send()

    def drain(i, carry):
        way = lax.rem(i, 2)
        sign = 1 - 2 * way
        level = z - sign * (lax.div(i, 2) + 1)
        following = z + sign

        @pl.when(jnp.logical_and(level >= 0, level < levels))
        def _():
            @pl.when(jnp.logical_and(following >= 0, following < levels))
            def _():
                target = following * CORES + core
                z_acts(level, way, target).wait_send()
                for g in range(CHUNKS):
                    z_grads(level, way, target, g).wait_send()

            for j in range(1, narrow):
                plane_acts(level, me, lax.rem(me + j, narrow)).wait_send()
            for n in range(narrow):
                core_acts(level, n, core).wait_send()
            for g in range(CHUNKS):
                core_grads(level, g, core).wait_send()

        return carry

    lax.fori_loop(0, 2 * (levels - 1), drain, 0)
    for j in range(1, narrow):
        sums(me, lax.rem(me + j, narrow)).wait_recv()
    raw = parts[0]
    for n in range(1, narrow):
        raw += parts[n]
    raw_out[...] = raw
    for j in range(1, narrow):
        sums(lax.rem(me + j, narrow), me).wait_send()


def body(query_left, query_right, acts, grads, order):
    queries, _, ranks, width = query_left.shape
    block = query_right.shape[2]
    rows = queries * ranks
    owners, narrow = lax.axis_size("wide"), lax.axis_size("narrow")
    levels = owners // CORES
    tokens = acts.shape[1]
    dma = pltpu.SemaphoreType.DMA
    hbm = pl.BlockSpec(memory_space=pl.ANY)
    raw = pl.pallas_call(
        functools.partial(kernel, levels, narrow),
        out_shape=jax.ShapeDtypeStruct((queries, 128), jnp.float32),
        in_specs=[hbm] * 4,
        out_specs=pl.BlockSpec(memory_space=pltpu.VMEM),
        scratch_shapes=[
            pltpu.VMEM((owners, tokens, width), jnp.bfloat16),
            pltpu.VMEM((owners, tokens, block), jnp.bfloat16),
            pltpu.VMEM((rows, width), jnp.float32),
            pltpu.VMEM((rows, block), jnp.float32),
            pltpu.VMEM((2 * rows, width), jnp.bfloat16),
            pltpu.VMEM((2 * rows, block), jnp.bfloat16),
            pltpu.VMEM((2, rows, CORES * tokens), jnp.float32),
            pltpu.VMEM((queries, 128), jnp.float32),
            pltpu.VMEM((narrow, queries, 128), jnp.float32),
            dma((4,)),
            dma((levels, 2)), dma((levels,)),
            dma((levels, 2, CHUNKS)), dma((levels, CHUNKS)),
            dma((levels, narrow)), dma((levels, narrow)),
            dma((levels, narrow)), dma((levels, narrow)),
            dma((levels, CHUNKS)), dma((levels, CHUNKS)),
            dma((narrow,)), dma((narrow,)),
        ],
        compiler_params=pltpu.CompilerParams(
            collective_id=0, has_side_effects=True, vmem_limit_bytes=58 * 1024 * 1024,
        ),
        cost_estimate=pl.CostEstimate(
            flops=4 * rows * owners * tokens * (width + block),
            bytes_accessed=4 * rows * (width + block), transcendentals=0,
        ),
        name="scores",
    )(
        query_left.reshape(rows, width),
        query_right.reshape(rows, block),
        acts,
        grads,
    )
    picker = (lax.broadcasted_iota(jnp.int32, (owners, owners), 0) == order[None, :]).astype(jnp.float32)
    return jnp.sum(raw[:, :owners, None] * picker[None], axis=1)


def solution(mesh):
    return jax.shard_map(
        body,
        mesh=mesh,
        in_specs=(
            P("wide", "narrow", None, None),
            P("wide", None, "narrow"),
            P("wide", None, None),
            P("wide", None, "narrow"),
            P(),
        ),
        out_specs=P("wide", None),
        check_vma=False,
    )
```

```python
import functools

import jax
import jax.numpy as jnp
from jax import lax
from jax.experimental import pallas as pl
from jax.experimental.pallas import tpu as pltpu
from jax.sharding import PartitionSpec as P

CORES = 2
CHUNKS = 4
MESH = pl.DeviceIdType.MESH


def kernel(
    levels, narrow, left_hbm, right_hbm, acts_hbm, grads_hbm, raw_out,
    acts_all, grads_all, left_in, right_in, left_two, right_two, x_ref, total, parts,
    load_sem, za_send, za_recv, zg_send, zg_recv, pa_send, pa_recv,
    ca_send, ca_recv, cg_send, cg_recv, sum_send, sum_recv,
):
    wide_at = lax.axis_index("wide")
    me = lax.axis_index("narrow")
    z = lax.div(wide_at, CORES)
    core = lax.rem(wide_at, CORES)
    other = z * CORES + (1 - core)
    tokens, width = acts_hbm.shape[1:]
    rows = left_hbm.shape[0]
    queries = raw_out.shape[0]
    ranks = rows // queries

    row_parts = min(narrow, tokens // 16)
    col_parts = narrow // row_parts
    piece_rows, piece_cols = tokens // row_parts, width // col_parts
    chunk_rows = tokens // CHUNKS

    def piece(n):
        row = pl.multiple_of(lax.rem(n, row_parts) * piece_rows, piece_rows)
        if col_parts == 1:
            return (pl.ds(row, piece_rows), slice(None))
        col = pl.multiple_of(lax.div(n, row_parts) * piece_cols, piece_cols)
        return (pl.ds(row, piece_rows), pl.ds(col, piece_cols))

    def acts_at(example, n):
        return acts_all.at[(example, *piece(n))]

    def grads_at(example, g):
        return grads_all.at[example, pl.ds(g * chunk_rows, chunk_rows), :]

    def send(src, dst, send_sem, recv_sem, **where):
        return pltpu.make_async_remote_copy(
            src_ref=src, dst_ref=dst, send_sem=send_sem, recv_sem=recv_sem,
            device_id=where, device_id_type=MESH,
        )

    def z_acts(level, way, target, src=None):
        slot = acts_at(level * CORES + core, me)
        return send(slot if src is None else src, slot, za_send.at[level, way], za_recv.at[level], wide=target)

    def z_grads(level, way, target, g, src=None):
        slot = grads_at(level * CORES + core, g)
        return send(slot if src is None else src, slot, zg_send.at[level, way, g], zg_recv.at[level, g], wide=target)

    def plane_acts(level, n, target):
        slot = acts_at(level * CORES + core, n)
        return send(slot, slot, pa_send.at[level, target], pa_recv.at[level, n], narrow=target)

    def core_acts(level, n, whose, src=None):
        slot = acts_at(level * CORES + whose, n)
        return send(slot if src is None else src, slot, ca_send.at[level, n], ca_recv.at[level, n], wide=other)

    def core_grads(level, g, whose, src=None):
        slot = grads_at(level * CORES + whose, g)
        return send(slot if src is None else src, slot, cg_send.at[level, g], cg_recv.at[level, g], wide=other)

    barrier = pltpu.get_barrier_semaphore()
    up, down = z + 1 < levels, z > 0

    @pl.when(up)
    def _():
        pl.semaphore_signal(barrier, inc=1, device_id={"wide": wide_at + CORES}, device_id_type=MESH)

    @pl.when(down)
    def _():
        pl.semaphore_signal(barrier, inc=1, device_id={"wide": wide_at - CORES}, device_id_type=MESH)

    pl.semaphore_signal(barrier, inc=1, device_id={"wide": other}, device_id_type=MESH)
    for j in range(1, narrow):
        pl.semaphore_signal(barrier, inc=1, device_id={"narrow": lax.rem(me + j, narrow)}, device_id_type=MESH)
    pl.semaphore_wait(barrier, narrow + up.astype(jnp.int32) + down.astype(jnp.int32))

    own_acts = acts_hbm.at[(0, *piece(me))]

    def own_grads(g):
        return grads_hbm.at[0, pl.ds(g * chunk_rows, chunk_rows), :]

    for way, ok in ((0, up), (1, down)):
        target = wide_at + (CORES if way == 0 else -CORES)

        @pl.when(ok)
        def _():
            z_acts(z, way, target, own_acts).start()
            for g in range(CHUNKS):
                z_grads(z, way, target, g, own_grads(g)).start()

    for n in range(narrow):
        core_acts(z, n, core, acts_hbm.at[(0, *piece(n))]).start()
    for g in range(CHUNKS):
        core_grads(z, g, core, own_grads(g)).start()

    loads = [
        pltpu.make_async_copy(left_hbm, left_in, load_sem.at[0]),
        pltpu.make_async_copy(right_hbm, right_in, load_sem.at[1]),
        pltpu.make_async_copy(acts_hbm.at[0], acts_all.at[wide_at], load_sem.at[2]),
        pltpu.make_async_copy(grads_hbm.at[0], grads_all.at[wide_at], load_sem.at[3]),
    ]
    for load in loads:
        load.start()
    total[...] = jnp.zeros_like(total)

    def split(src, dst):
        def step(i, carry):
            row = pl.multiple_of(i * 32, 32)
            value = src[pl.ds(row, 32), :]
            high = value.astype(jnp.bfloat16)
            dst[pl.ds(row, 32), :] = high
            dst[pl.ds(rows + row, 32), :] = (value - high.astype(jnp.float32)).astype(jnp.bfloat16)
            return carry

        lax.fori_loop(0, rows // 32, step, 0)

    loads[0].wait()
    split(left_in, left_two)
    loads[1].wait()
    split(right_in, right_two)
    loads[2].wait()
    loads[3].wait()

    def project(two, ref, level):
        block = ref[pl.ds(level * CORES, CORES)]
        block = block.reshape(CORES * tokens, block.shape[2])
        both = lax.dot_general(two[...], block, (((1,), (1,)), ((), ())), preferred_element_type=jnp.float32)
        return both[:rows] + both[rows:]

    def left_work(level, way):
        for n in range(narrow):
            core_acts(level, n, 1 - core).wait_recv()
        x_ref[way] = project(left_two, acts_all, level)

    def right_work(level, way):
        for g in range(CHUNKS):
            core_grads(level, g, 1 - core).wait_recv()
        product = x_ref[way] * project(right_two, grads_all, level)
        by_query = jnp.sum(product.reshape(queries, ranks, CORES * tokens), axis=1)
        column = lax.broadcasted_iota(jnp.int32, total.shape, 1)
        for c in range(CORES):
            score = jnp.sum(by_query[:, c * tokens:(c + 1) * tokens], axis=1, keepdims=True)
            total[...] += jnp.where(column == level * CORES + c, score, 0.0)

    def arrivals(d):
        found = []
        for way, sign in ((0, 1), (1, -1)):
            level, following = z - sign * d, z + sign
            valid = jnp.logical_and(level >= 0, level < levels)
            onward = jnp.logical_and(following >= 0, following < levels)
            found.append((way, level, valid, jnp.logical_and(valid, onward), following * CORES + core))
        return found

    def take_grads(now, g):
        for way, level, valid, onward, target in now:
            @pl.when(valid)
            def _():
                z_grads(level, way, wide_at, g).wait_recv()

            @pl.when(onward)
            def _():
                z_grads(level, way, target, g).start()

            @pl.when(valid)
            def _():
                core_grads(level, g, core).start()

    def step(i, carry):
        now = arrivals(i + 1)
        for way, level, valid, onward, target in now:
            @pl.when(valid)
            def _():
                z_acts(level, way, wide_at).wait_recv()

            @pl.when(onward)
            def _():
                z_acts(level, way, target).start()

            @pl.when(valid)
            def _():
                for j in range(1, narrow):
                    plane_acts(level, me, lax.rem(me + j, narrow)).start()
                core_acts(level, me, core).start()

        take_grads(now, 0)
        take_grads(now, 1)
        for way, level, valid, _, _ in now:
            @pl.when(valid)
            def _():
                for j in range(1, narrow):
                    n = lax.rem(me + j, narrow)
                    plane_acts(level, n, me).wait_recv()
                    core_acts(level, n, core).start()

        take_grads(now, 2)
        for way, level, valid, _, _ in now:
            @pl.when(jnp.logical_and(valid, i == levels - 2))
            def _():
                left_work(level, way)

        for g in range(3, CHUNKS):
            take_grads(now, g)
        for way, level, valid, _, _ in now:
            @pl.when(jnp.logical_and(valid, i < levels - 2))
            def _():
                left_work(level, way)
                right_work(level, way)

        return carry

    left_work(z, 0)
    right_work(z, 0)
    lax.fori_loop(0, levels - 1, step, 0)
    for way, level, valid, _, _ in arrivals(levels - 1):
        @pl.when(valid)
        def _():
            right_work(level, way)

    parts[me] = total[...]

    def sums(target, n):
        return send(total, parts.at[n], sum_send.at[target], sum_recv.at[n], narrow=target)

    for j in range(1, narrow):
        sums(lax.rem(me + j, narrow), me).start()

    for n in range(narrow):
        core_acts(z, n, core).wait_send()
    for g in range(CHUNKS):
        core_grads(z, g, core).wait_send()
    for way, ok in ((0, up), (1, down)):
        target = wide_at + (CORES if way == 0 else -CORES)

        @pl.when(ok)
        def _():
            z_acts(z, way, target).wait_send()
            for g in range(CHUNKS):
                z_grads(z, way, target, g).wait_send()

    def drain(i, carry):
        way = lax.rem(i, 2)
        sign = 1 - 2 * way
        level = z - sign * (lax.div(i, 2) + 1)
        following = z + sign

        @pl.when(jnp.logical_and(level >= 0, level < levels))
        def _():
            @pl.when(jnp.logical_and(following >= 0, following < levels))
            def _():
                target = following * CORES + core
                z_acts(level, way, target).wait_send()
                for g in range(CHUNKS):
                    z_grads(level, way, target, g).wait_send()

            for j in range(1, narrow):
                plane_acts(level, me, lax.rem(me + j, narrow)).wait_send()
            for n in range(narrow):
                core_acts(level, n, core).wait_send()
            for g in range(CHUNKS):
                core_grads(level, g, core).wait_send()

        return carry

    lax.fori_loop(0, 2 * (levels - 1), drain, 0)
    for j in range(1, narrow):
        sums(me, lax.rem(me + j, narrow)).wait_recv()
    raw = parts[0]
    for n in range(1, narrow):
        raw += parts[n]
    raw_out[...] = raw
    for j in range(1, narrow):
        sums(lax.rem(me + j, narrow), me).wait_send()


def body(query_left, query_right, acts, grads, order):
    queries, _, ranks, width = query_left.shape
    block = query_right.shape[2]
    rows = queries * ranks
    owners, narrow = lax.axis_size("wide"), lax.axis_size("narrow")
    levels = owners // CORES
    tokens = acts.shape[1]
    dma = pltpu.SemaphoreType.DMA
    hbm = pl.BlockSpec(memory_space=pl.ANY)
    raw = pl.pallas_call(
        functools.partial(kernel, levels, narrow),
        out_shape=jax.ShapeDtypeStruct((queries, 128), jnp.float32),
        in_specs=[hbm] * 4,
        out_specs=pl.BlockSpec(memory_space=pltpu.VMEM),
        scratch_shapes=[
            pltpu.VMEM((owners, tokens, width), jnp.bfloat16),
            pltpu.VMEM((owners, tokens, block), jnp.bfloat16),
            pltpu.VMEM((rows, width), jnp.float32),
            pltpu.VMEM((rows, block), jnp.float32),
            pltpu.VMEM((2 * rows, width), jnp.bfloat16),
            pltpu.VMEM((2 * rows, block), jnp.bfloat16),
            pltpu.VMEM((2, rows, CORES * tokens), jnp.float32),
            pltpu.VMEM((queries, 128), jnp.float32),
            pltpu.VMEM((narrow, queries, 128), jnp.float32),
            dma((4,)),
            dma((levels, 2)), dma((levels,)),
            dma((levels, 2, CHUNKS)), dma((levels, CHUNKS)),
            dma((levels, narrow)), dma((levels, narrow)),
            dma((levels, narrow)), dma((levels, narrow)),
            dma((levels, CHUNKS)), dma((levels, CHUNKS)),
            dma((narrow,)), dma((narrow,)),
        ],
        compiler_params=pltpu.CompilerParams(
            collective_id=0, has_side_effects=True, vmem_limit_bytes=58 * 1024 * 1024,
        ),
        cost_estimate=pl.CostEstimate(
            flops=4 * rows * owners * tokens * (width + block),
            bytes_accessed=4 * rows * (width + block), transcendentals=0,
        ),
        name="scores",
    )(
        query_left.reshape(rows, width),
        query_right.reshape(rows, block),
        acts,
        grads,
    )
    picker = (lax.broadcasted_iota(jnp.int32, (owners, owners), 0) == order[None, :]).astype(jnp.float32)
    return jnp.sum(raw[:, :owners, None] * picker[None], axis=1)


def solution(mesh):
    return jax.shard_map(
        body,
        mesh=mesh,
        in_specs=(
            P("wide", "narrow", None, None),
            P("wide", None, "narrow"),
            P("wide", None, None),
            P("wide", None, "narrow"),
            P(),
        ),
        out_specs=P("wide", None),
        check_vma=False,
    )
```
